32 devices in a mesh: seq: 8 (over y, x, core), head: 4 (over z).
Axes of the slice: x: 2, y: 2, z: 4, core: 2. Of those that a mesh axis runs over, the one named last changes fastest.
Arguments:
- queries: bfloat16 [3072, 1024], P('seq', 'head'), may hold values from -6 to 6
- key_rows: bfloat16 [3072, 1024], P('seq', 'head'), may hold values from -6 to 6
- value_rows: bfloat16 [3072, 1024], P('seq', 'head'), may hold values from -6 to 6
- out_weight: bfloat16 [4096, 1024], P(None, 'head'), may hold values from -0.1875 to 0.1875
- out_grad: bfloat16 [3072, 4096], P('seq'), may hold values from -6 to 6
Outputs:
- output: bfloat16 [3072, 4096], P(('seq', 'head'))
- query_grad: bfloat16 [3072, 1024], P('seq', 'head')
- key_grad: bfloat16 [3072, 1024], P('seq', 'head')
- value_grad: bfloat16 [3072, 1024], P('seq', 'head')
- weight_grad: float32 [4096, 1024], P('seq', 'head')
The draws below stay inside these ranges and needn't reach their ends.
All inputs are finite; a program needn't handle non-finite values.
Results may differ from the reference program's by a relative error of at most 0.02.
Values may be sent and summed in bfloat16 or wider, within the bound.
A program may use at most 64 MiB of HBM per device.

```python
import jax
import jax.numpy as jnp
from jax import lax

D = 4096
HD = 128
CH = 64
HEAD_DEV = 2
HEADS = 8
INNER = 1024
TOKENS = 3072
N_HEAD = 4


def strengthened(array, own_key, source, target, parts, factor):
    owner, partner = [(jnp.arange(array.shape[axis_at]) // (array.shape[axis_at] // parts)).reshape([-1 if axis == axis_at else 1 for axis in range(array.ndim)]) for axis_at in (source, target)]
    chosen = jax.random.permutation(own_key, parts)[partner]
    strong = (owner == chosen) | (owner == (partner + parts // 2) % parts)
    return jnp.where(strong, factor * array, array)


def shard_levels(rng, shape, split, least, top_value):
    def one(dim, parts):
        heights = jax.random.uniform(jax.random.fold_in(jax.random.fold_in(rng, 6), dim), (parts,), jnp.float32, least / len(split), top_value / len(split))
        return jnp.repeat(jnp.exp(heights), shape[dim] // parts).reshape((-1,) + (1,) * (len(shape) - dim - 1))

    level = one(*split[0])
    for cut in split[1:]:
        level = level * one(*cut)
    return level


def noise(own_key, shape, width, limit, pieces=(), held_as=jnp.bfloat16):
    array = width * jax.random.normal(own_key, shape, jnp.float32)
    if pieces:
        array = array * shard_levels(own_key, shape, pieces, -0.22, 0.18)
    return jnp.clip(array, -limit, limit).astype(held_as)


def bell_draw_with(own_key, dims, width, limit, cuts, heavy, kind=jnp.bfloat16):
    drawn = width * jax.random.normal(own_key, dims, jnp.float32)
    if cuts:
        drawn = drawn * shard_levels(own_key, dims, cuts, -0.22, 0.18)
    return jnp.clip(strengthened(drawn, jax.random.fold_in(own_key, 3), *heavy), -limit, limit).astype(kind)


def setup_inputs(seed: int = 0) -> dict:
    arg_keys = jax.random.split(jax.random.key(seed), 6)
    queries = noise(arg_keys[0], (TOKENS, INNER), 1.0, 6.0, ((0, 8), (1, 4)))
    key_rows = noise(arg_keys[1], (TOKENS, INNER), 1.0, 6.0, ((0, 8), (1, 4)))
    value_rows = noise(arg_keys[2], (TOKENS, INNER), 1.0, 6.0, ((0, 8), (1, 4)))
    out_weight = noise(arg_keys[3], (D, INNER), INNER ** -0.5, 0.1875, ((1, 4),))
    out_grad = bell_draw_with(arg_keys[4], (TOKENS, D), 1.0, 6.0, ((0, 8),), (0, 1, 8, 2.0))
    return dict(queries=queries, key_rows=key_rows, value_rows=value_rows, out_weight=out_weight, out_grad=out_grad)


def rounded(values):
    return lax.optimization_barrier(values.astype(jnp.bfloat16)).astype(jnp.float32)


def reference(queries, key_rows, value_rows, out_weight, out_grad):
    factor = (HD * TOKENS) ** -0.5
    blocks = TOKENS // CH
    highest = lax.Precision.HIGHEST
    causal = (jnp.arange(CH)[:, None] >= jnp.arange(CH)[None, :]).astype(jnp.float32)
    grad_rows = jnp.dot(out_grad, out_weight, preferred_element_type=jnp.float32).astype(jnp.bfloat16)
    attn_list = []
    qgrad_list = []
    kgrad_list = []
    vgrad_list = []
    for head_index in range(HEADS):
        low = head_index * HD
        query_part = queries[:, low:low + HD].astype(jnp.float32).reshape(blocks, CH, HD)
        key_part = key_rows[:, low:low + HD].astype(jnp.float32).reshape(blocks, CH, HD)
        value_part = value_rows[:, low:low + HD].astype(jnp.float32).reshape(blocks, CH, HD)
        grad_part = grad_rows[:, low:low + HD].astype(jnp.float32).reshape(blocks, CH, HD)
        scores = jnp.einsum('ctd,csd->cts', query_part, key_part, precision=highest)
        weights = rounded(factor * scores * causal)
        key_value = jnp.einsum('csd,cse->cde', key_part, value_part, precision=highest)
        before = jnp.cumsum(key_value, 0) - key_value
        within = jnp.einsum('cts,cse->cte', weights, value_part, precision=highest)
        carried = factor * jnp.einsum('ctd,cde->cte', query_part, before, precision=highest)
        attn_list.append((within + carried).astype(jnp.bfloat16).reshape(TOKENS, HD))
        grad_weights = rounded(factor * jnp.einsum('cte,cse->cts', grad_part, value_part, precision=highest) * causal)
        query_pairs = jnp.einsum('ctd,cte->cde', query_part, grad_part, precision=highest)
        later_state = jnp.flip(jnp.cumsum(jnp.flip(query_pairs, 0), 0), 0) - query_pairs
        query_grad = jnp.einsum('cts,csd->ctd', grad_weights, key_part, precision=highest)
        query_grad = query_grad + factor * jnp.einsum('cte,cde->ctd', grad_part, before, precision=highest)
        key_grad = jnp.einsum('cts,ctd->csd', grad_weights, query_part, precision=highest)
        key_grad = key_grad + factor * jnp.einsum('cse,cde->csd', value_part, later_state, precision=highest)
        value_grad = jnp.einsum('cts,cte->cse', weights, grad_part, precision=highest)
        value_grad = value_grad + factor * jnp.einsum('csd,cde->cse', key_part, later_state, precision=highest)
        qgrad_list.append(query_grad.astype(jnp.bfloat16).reshape(TOKENS, HD))
        kgrad_list.append(key_grad.astype(jnp.bfloat16).reshape(TOKENS, HD))
        vgrad_list.append(value_grad.astype(jnp.bfloat16).reshape(TOKENS, HD))
    attention = jnp.concatenate(attn_list, 1)
    group_width = HEAD_DEV * HD
    summed = jnp.zeros((TOKENS, D), jnp.float32)
    for group_index in range(N_HEAD):
        low = group_index * group_width
        partial_product = jnp.dot(attention[:, low:low + group_width], out_weight[:, low:low + group_width].T, preferred_element_type=jnp.float32)
        summed = summed + rounded(partial_product)
    output = summed.astype(jnp.bfloat16)
    weight_grad = jnp.dot(out_grad.T, attention, preferred_element_type=jnp.float32) * (TOKENS ** -0.5)
    return (output, jnp.concatenate(qgrad_list, 1), jnp.concatenate(kgrad_list, 1), jnp.concatenate(vgrad_list, 1), weight_grad)
```

```python
import functools

import jax
import jax.numpy as jnp
from jax import lax
from jax.experimental import pallas as pl
from jax.experimental.pallas import tpu as pltpu
from jax.sharding import PartitionSpec as P

HD = 128
CH = 64


def swapped(block, axis, distance):
    count = lax.axis_size(axis)
    route = []
    for low in range(count):
        high = low | 1 << distance
        if high != low and high < count:
            route += [(low, high), (high, low)]
    return lax.ppermute(block, axis, route)


def split_state(state):
    upper = state.astype(jnp.bfloat16)
    lower = (state - upper.astype(jnp.float32)).astype(jnp.bfloat16)
    return (upper, lower)


def state_product(form, operand, parts):
    first = jnp.einsum(form, operand, parts[0], preferred_element_type=jnp.float32)
    return first + jnp.einsum(form, operand, parts[1], preferred_element_type=jnp.float32)


def local(queries, key_rows, value_rows, out_weight, out_grad):
    local_rows = queries.shape[0]
    head_count = queries.shape[1] // HD
    blocks = local_rows // CH
    total_rows = local_rows * lax.axis_size("seq")
    factor = (HD * total_rows) ** (-0.5)
    block_shape = (blocks, CH, head_count, HD)
    flat_shape = (local_rows, head_count * HD)
    query_blocks = queries.reshape(block_shape)
    key_blocks = key_rows.reshape(block_shape)
    value_blocks = value_rows.reshape(block_shape)
    causal = (jnp.arange(CH)[:, None] >= jnp.arange(CH)[None, :])[None, None]
    grad_rows = jnp.dot(out_grad, out_weight, preferred_element_type=jnp.float32).astype(
        jnp.bfloat16
    )
    grad_blocks = grad_rows.reshape(block_shape)
    key_value = jnp.einsum(
        "cshd,cshe->chde", key_blocks, value_blocks, preferred_element_type=jnp.float32
    )
    query_pairs = jnp.einsum(
        "cthd,cthe->chde", query_blocks, grad_blocks, preferred_element_type=jnp.float32
    )
    own_state = jnp.sum(key_value, 0)
    own_pairs = jnp.sum(query_pairs, 0)
    empty_state = jnp.zeros_like(own_state)
    position = lax.axis_index("seq")
    level_count = lax.axis_size("seq").bit_length() - 1
    inflow = empty_state
    outflow = empty_state
    state_total = own_state
    pairs_total = own_pairs
    for level in range(level_count):
        other_state, other_pairs = (
            swapped(state_total.astype(jnp.bfloat16), "seq", level).astype(state_total.dtype),
            swapped(pairs_total.astype(jnp.bfloat16), "seq", level).astype(pairs_total.dtype),
        )
        upper_half = position >> level & 1 == 1
        inflow = inflow + jnp.where(upper_half, other_state, 0.0)
        outflow = outflow + jnp.where(upper_half, 0.0, other_pairs)
        state_total = state_total + other_state
        pairs_total = pairs_total + other_pairs
    before = inflow[None] + jnp.cumsum(key_value, 0) - key_value
    later_state = outflow[None] + own_pairs[None] - jnp.cumsum(query_pairs, 0)
    before_parts = split_state(before)
    later_parts = split_state(later_state)
    scores = jnp.einsum(
        "cthd,cshd->chts", query_blocks, key_blocks, preferred_element_type=jnp.float32
    )
    weights = jnp.where(causal, factor * scores, 0.0).astype(jnp.bfloat16)
    within = jnp.einsum(
        "chts,cshe->cthe", weights, value_blocks, preferred_element_type=jnp.float32
    )
    carried = factor * state_product("cthd,chde->cthe", query_blocks, before_parts)
    attention = (within + carried).astype(jnp.bfloat16).reshape(flat_shape)
    output = lax.psum_scatter(
        lax.dot_general(
            attention, out_weight, (((1,), (1,)), ((), ())), preferred_element_type=jnp.float32
        ).astype(jnp.bfloat16),
        "head",
        scatter_dimension=0,
        tiled=True,
    )
    grad_scores = jnp.einsum(
        "cthe,cshe->chts", grad_blocks, value_blocks, preferred_element_type=jnp.float32
    )
    grad_weights = jnp.where(causal, factor * grad_scores, 0.0).astype(jnp.bfloat16)
    query_grad = jnp.einsum(
        "chts,cshd->cthd", grad_weights, key_blocks, preferred_element_type=jnp.float32
    )
    query_grad = query_grad + factor * state_product("cthe,chde->cthd", grad_blocks, before_parts)
    key_grad = jnp.einsum(
        "chts,cthd->cshd", grad_weights, query_blocks, preferred_element_type=jnp.float32
    )
    key_grad = key_grad + factor * state_product("cshe,chde->cshd", value_blocks, later_parts)
    value_grad = jnp.einsum(
        "chts,cthe->cshe", weights, grad_blocks, preferred_element_type=jnp.float32
    )
    value_grad = value_grad + factor * state_product("cshd,chde->cshe", key_blocks, later_parts)
    weight_grad = lax.psum_scatter(
        lax.dot_general(
            out_grad, attention, (((0,), (0,)), ((), ())), preferred_element_type=jnp.float32
        ),
        "seq",
        scatter_dimension=0,
        tiled=True,
    ) * total_rows ** (-0.5)
    return (
        output,
        query_grad.astype(jnp.bfloat16).reshape(flat_shape),
        key_grad.astype(jnp.bfloat16).reshape(flat_shape),
        value_grad.astype(jnp.bfloat16).reshape(flat_shape),
        weight_grad,
    )


def flipped(position, mask):
    result = position
    for bit in range(mask.bit_length()):
        if mask >> bit & 1:
            step = 1 << bit
            result = result + (1 - 2 * (position // step % 2)) * step
    return result


def nn(a, b):
    return jnp.dot(a, b, preferred_element_type=jnp.float32)


def nt(a, b):
    return lax.dot_general(a, b, (((1,), (1,)), ((), ())), preferred_element_type=jnp.float32)


def tn(a, b):
    return lax.dot_general(a, b, (((0,), (0,)), ((), ())), preferred_element_type=jnp.float32)


def fused_kernel(
    n_seq, n_head, q_ref, k_ref, v_ref, w_ref, og_ref,
    out_ref, qg_ref, kg_ref, vg_ref, wg_ref,
    wf, state_out, state_in, grad, att, att_t, att_in, acc,
    part_out, part_in, sum_out, sum_in,
    z_send, z_recv, p_send, p_recv, c_send, c_recv,
    s_send, s_recv, a_send, a_recv, g_send, g_recv, r_send, r_recv,
):
    rows = q_ref.shape[0]
    width = w_ref.shape[0]
    heads = q_ref.shape[1] // HD
    chips = n_seq // 2
    block = width // n_seq
    mine = rows // n_head
    total_rows = rows * n_seq
    factor = (HD * total_rows) ** (-0.5)
    seq = lax.axis_index("seq")
    z = lax.axis_index("head")
    chip = seq // 2
    core = seq % 2
    partner = chip * 2 + 1 - core

    def zpeer(dz):
        return lax.rem(z + dz, n_head)

    def peer_chip(k):
        return flipped(chip, k)

    def band(j):
        return pl.ds(pl.multiple_of(j * block, block), block)

    def remote(src, dst, send, recv, **where):
        return pltpu.make_async_remote_copy(
            src_ref=src, dst_ref=dst, send_sem=send, recv_sem=recv,
            device_id=where, device_id_type=pl.DeviceIdType.MESH,
        )

    barrier = pltpu.get_barrier_semaphore()
    for m in range(1, n_seq):
        pl.semaphore_signal(
            barrier, inc=1, device_id={"seq": flipped(seq, m)},
            device_id_type=pl.DeviceIdType.MESH,
        )
    for dz in range(1, n_head):
        pl.semaphore_signal(
            barrier, inc=1, device_id={"head": zpeer(dz)},
            device_id_type=pl.DeviceIdType.MESH,
        )
    pl.semaphore_wait(barrier, n_seq + n_head - 2)

    def z_copy(dz):
        back = n_head - dz
        return remote(
            w_ref.at[band(seq)], wf.at[back - 1, band(seq)],
            z_send.at[dz - 1], z_recv.at[back - 1], head=zpeer(dz),
        )

    def z_wait(dz):
        return remote(
            w_ref.at[band(seq)], wf.at[dz - 1, band(seq)],
            z_send.at[dz - 1], z_recv.at[dz - 1], head=zpeer(dz),
        )

    for dz in range(1, n_head):
        z_copy(dz).start()

    def state_copy(m, which):
        return remote(
            state_out.at[which], state_in.at[m - 1],
            s_send.at[m - 1], s_recv.at[m - 1], seq=flipped(seq, m),
        )

    for h in range(heads):
        cols = pl.ds(h * HD, HD)
        state_out[0, h] = tn(k_ref[:, cols], v_ref[:, cols]).astype(jnp.bfloat16)
    for m in range(1, n_seq):
        @pl.when(flipped(seq, m) > seq)
        def _():
            state_copy(m, 0).start()

    acc[0] = jnp.zeros(acc.shape[1:], jnp.float32)

    @pl.loop(0, n_seq)
    def _(j):
        acc[0] += nn(og_ref[:, band(j)], w_ref[band(j), :])

    grad[...] = acc[0].astype(jnp.bfloat16)
    for h in range(heads):
        cols = pl.ds(h * HD, HD)
        state_out[1, h] = tn(q_ref[:, cols], grad[:, cols]).astype(jnp.bfloat16)
    for m in range(1, n_seq):
        @pl.when(flipped(seq, m) < seq)
        def _():
            state_copy(m, 1).start()

    row = lax.broadcasted_iota(jnp.int32, (rows, rows), 0)
    col = lax.broadcasted_iota(jnp.int32, (rows, rows), 1)
    for h in range(heads):
        cols = pl.ds(h * HD, HD)
        q, k, v, g = q_ref[:, cols], k_ref[:, cols], v_ref[:, cols], grad[:, cols]
        weights = jnp.where(row >= col, factor * nt(q, k), 0.0).astype(jnp.bfloat16)
        acc[0, :, cols] = nn(weights, v)
        weights = jnp.where(row >= col, factor * nt(g, v), 0.0).astype(jnp.bfloat16)
        acc[1, :, cols] = nn(weights, k)
        weights = jnp.where(row <= col, factor * nt(v, g), 0.0).astype(jnp.bfloat16)
        acc[2, :, cols] = nn(weights, q)
        weights = jnp.where(row <= col, factor * nt(k, q), 0.0).astype(jnp.bfloat16)
        acc[3, :, cols] = nn(weights, g)

    inflow = jnp.zeros(state_out.shape[1:], jnp.float32)
    outflow = inflow
    for m in range(1, n_seq):
        state_copy(m, 0).wait_recv()
        arrived = state_in[m - 1].astype(jnp.float32)
        early = (flipped(seq, m) < seq).astype(jnp.float32)
        inflow = inflow + early * arrived
        outflow = outflow + (1.0 - early) * arrived
    inflow = inflow.astype(jnp.bfloat16)
    outflow = outflow.astype(jnp.bfloat16)
    for h in range(heads):
        cols = pl.ds(h * HD, HD)
        full = acc[0, :, cols] + factor * nn(q_ref[:, cols], inflow[h])
        att[:, cols] = full.astype(jnp.bfloat16)
        att_t[cols, :] = full.T.astype(jnp.bfloat16)

    def att_copy(dz):
        back = n_head - dz
        start = pl.multiple_of(zpeer(dz) * mine, mine)
        return remote(
            att.at[pl.ds(start, mine)], att_in.at[back - 1],
            a_send.at[dz - 1], a_recv.at[back - 1], head=zpeer(dz),
        )

    for dz in range(1, n_head):
        att_copy(dz).start()

    def share(j):
        return nn(att_t[...], og_ref[:, band(j)])

    def part_copy(k):
        return remote(
            part_out.at[k], part_in.at[k], g_send.at[k], g_recv.at[k], seq=partner
        )

    def sum_copy(k):
        return remote(
            sum_out.at[k - 1], sum_in.at[k - 1], r_send.at[k - 1], r_recv.at[k - 1],
            seq=peer_chip(k) * 2 + core,
        )

    order = list(range(1, chips))[::-1] + [0]
    for k in order:
        part_out[k] = share(peer_chip(k) * 2 + 1 - core).astype(jnp.bfloat16)
        part_copy(k).start()

    def p_copy(dz, k):
        at = (dz - 1) * chips + k
        return remote(
            wf.at[dz - 1, band(seq)], wf.at[dz - 1, band(seq)],
            p_send.at[at], p_recv.at[at], seq=peer_chip(k) * 2 + core,
        )

    def p_wait(dz, k):
        at = (dz - 1) * chips + k
        there = band(peer_chip(k) * 2 + core)
        return remote(
            wf.at[dz - 1, there], wf.at[dz - 1, there],
            p_send.at[at], p_recv.at[at], seq=peer_chip(k) * 2 + core,
        )

    def c_copy(dz, k, side):
        at = (dz - 1) * chips + k
        there = band(peer_chip(k) * 2 + side)
        return remote(
            wf.at[dz - 1, there], wf.at[dz - 1, there],
            c_send.at[at], c_recv.at[at], seq=partner,
        )

    hops = [1, 3, 2] if n_head == 4 else list(range(1, n_head))

    def forward(dz):
        z_wait(dz).wait_recv()
        for k in range(chips - 1, 0, -1):
            p_copy(dz, k).start()
        c_copy(dz, 0, core).start()

    forward(hops[0])
    own = None
    for k in order:
        part_copy(k).wait_recv()
        total = share(peer_chip(k) * 2 + core) + part_in[k].astype(jnp.float32)
        if k:
            sum_out[k - 1] = total.astype(jnp.bfloat16)
            sum_copy(k).start()
        else:
            wg_ref[...] = total
    for dz in hops[1:]:
        forward(dz)

    for h in range(heads):
        cols = pl.ds(h * HD, HD)
        q, k, v, g = q_ref[:, cols], k_ref[:, cols], v_ref[:, cols], grad[:, cols]
        qg_ref[:, cols] = (acc[1, :, cols] + factor * nt(g, inflow[h])).astype(jnp.bfloat16)
        kg_ref[:, cols] = (acc[2, :, cols] + factor * nt(v, outflow[h])).astype(jnp.bfloat16)
        vg_ref[:, cols] = (acc[3, :, cols] + factor * nn(k, outflow[h])).astype(jnp.bfloat16)

    for k in range(1, chips):
        sum_copy(k).wait_recv()
        wg_ref[...] += sum_in[k - 1].astype(jnp.float32)
    wg_ref[...] = wg_ref[...] * total_rows ** (-0.5)

    for dz in range(1, n_head):
        att_copy(n_head - dz).wait_recv()

    for dz in hops:
        for k in range(1, chips):
            p_wait(dz, k).wait_recv()
            c_copy(dz, k, core).start()

    at_home = pl.ds(pl.multiple_of(z * mine, mine), mine)

    def finish(j):
        there = band(j)
        total = nt(att[at_home, :], w_ref[there, :]).astype(jnp.bfloat16).astype(jnp.float32)
        for dz in range(1, n_head):
            term = nt(att_in[dz - 1], wf[dz - 1, there, :])
            total = total + term.astype(jnp.bfloat16).astype(jnp.float32)
        out_ref[:, there] = total.astype(jnp.bfloat16)

    @pl.loop(0, chips)
    def _(p):
        finish(p * 2 + core)

    for dz in hops:
        for k in range(chips):
            c_copy(dz, k, 1 - core).wait_recv()

    @pl.loop(0, chips)
    def _(p):
        finish(p * 2 + 1 - core)

    for dz in range(1, n_head):
        z_copy(dz).wait_send()
        att_copy(dz).wait_send()
        for k in range(chips):
            if k:
                p_copy(dz, k).wait_send()
            c_copy(dz, k, core).wait_send()
    for m in range(1, n_seq):
        state_copy(m, 0).wait_send()
    for k in range(chips):
        part_copy(k).wait_send()
        if k:
            sum_copy(k).wait_send()


def fused(n_seq, n_head, queries, key_rows, value_rows, out_weight, out_grad):
    rows, inner = queries.shape
    width = out_weight.shape[0]
    heads = inner // HD
    chips = n_seq // 2
    block = width // n_seq
    mine = rows // n_head
    bf = jnp.bfloat16
    vmem = pl.BlockSpec(memory_space=pltpu.VMEM)

    def sems(count):
        return pltpu.SemaphoreType.DMA((count,))

    others = n_head - 1
    output, query_grad, key_grad, value_grad, weight_grad = pl.pallas_call(
        functools.partial(fused_kernel, n_seq, n_head),
        out_shape=(
            jax.ShapeDtypeStruct((mine, width), bf),
            jax.ShapeDtypeStruct((rows, inner), bf),
            jax.ShapeDtypeStruct((rows, inner), bf),
            jax.ShapeDtypeStruct((rows, inner), bf),
            jax.ShapeDtypeStruct((inner, block), jnp.float32),
        ),
        in_specs=[vmem] * 5,
        out_specs=(vmem,) * 5,
        scratch_shapes=[
            pltpu.VMEM((others, width, inner), bf),
            pltpu.VMEM((2, heads, HD, HD), bf),
            pltpu.VMEM((n_seq - 1, heads, HD, HD), bf),
            pltpu.VMEM((rows, inner), bf),
            pltpu.VMEM((rows, inner), bf),
            pltpu.VMEM((inner, rows), bf),
            pltpu.VMEM((others, mine, inner), bf),
            pltpu.VMEM((4, rows, inner), jnp.float32),
            pltpu.VMEM((chips, inner, block), bf),
            pltpu.VMEM((chips, inner, block), bf),
            pltpu.VMEM((chips - 1, inner, block), bf),
            pltpu.VMEM((chips - 1, inner, block), bf),
            sems(others), sems(others),
            sems(others * chips), sems(others * chips),
            sems(others * chips), sems(others * chips),
            sems(n_seq - 1), sems(n_seq - 1),
            sems(others), sems(others),
            sems(chips), sems(chips),
            sems(chips - 1), sems(chips - 1),
        ],
        compiler_params=pltpu.CompilerParams(
            collective_id=0, has_side_effects=True, vmem_limit_bytes=44 << 20
        ),
    )(queries, key_rows, value_rows, out_weight, out_grad)
    return output, query_grad, key_grad, value_grad, weight_grad.T


def solution(mesh):
    sizes = (mesh.shape["seq"], mesh.shape["head"])
    body = functools.partial(fused, *sizes) if sizes == (8, 4) else local
    return jax.shard_map(
        body,
        mesh=mesh,
        in_specs=(
            P("seq", "head"),
            P("seq", "head"),
            P("seq", "head"),
            P(None, "head"),
            P("seq", None),
        ),
        out_specs=(
            P(("seq", "head"), None),
            P("seq", "head"),
            P("seq", "head"),
            P("seq", "head"),
            P("seq", "head"),
        ),
        check_vma=False,
    )
```

```python
import functools

import jax
import jax.numpy as jnp
from jax import lax
from jax.experimental import pallas as pl
from jax.experimental.pallas import tpu as pltpu
from jax.sharding import PartitionSpec as P

HD = 128
CH = 64


def swapped(block, axis, distance):
    count = lax.axis_size(axis)
    route = []
    for low in range(count):
        high = low | 1 << distance
        if high != low and high < count:
            route += [(low, high), (high, low)]
    return lax.ppermute(block, axis, route)


def split_state(state):
    upper = state.astype(jnp.bfloat16)
    lower = (state - upper.astype(jnp.float32)).astype(jnp.bfloat16)
    return (upper, lower)


def state_product(form, operand, parts):
    first = jnp.einsum(form, operand, parts[0], preferred_element_type=jnp.float32)
    return first + jnp.einsum(form, operand, parts[1], preferred_element_type=jnp.float32)


def local(queries, key_rows, value_rows, out_weight, out_grad):
    local_rows = queries.shape[0]
    head_count = queries.shape[1] // HD
    blocks = local_rows // CH
    total_rows = local_rows * lax.axis_size("seq")
    factor = (HD * total_rows) ** (-0.5)
    block_shape = (blocks, CH, head_count, HD)
    flat_shape = (local_rows, head_count * HD)
    query_blocks = queries.reshape(block_shape)
    key_blocks = key_rows.reshape(block_shape)
    value_blocks = value_rows.reshape(block_shape)
    causal = (jnp.arange(CH)[:, None] >= jnp.arange(CH)[None, :])[None, None]
    grad_rows = jnp.dot(out_grad, out_weight, preferred_element_type=jnp.float32).astype(
        jnp.bfloat16
    )
    grad_blocks = grad_rows.reshape(block_shape)
    key_value = jnp.einsum(
        "cshd,cshe->chde", key_blocks, value_blocks, preferred_element_type=jnp.float32
    )
    query_pairs = jnp.einsum(
        "cthd,cthe->chde", query_blocks, grad_blocks, preferred_element_type=jnp.float32
    )
    own_state = jnp.sum(key_value, 0)
    own_pairs = jnp.sum(query_pairs, 0)
    empty_state = jnp.zeros_like(own_state)
    position = lax.axis_index("seq")
    level_count = lax.axis_size("seq").bit_length() - 1
    inflow = empty_state
    outflow = empty_state
    state_total = own_state
    pairs_total = own_pairs
    for level in range(level_count):
        other_state, other_pairs = (
            swapped(state_total.astype(jnp.bfloat16), "seq", level).astype(state_total.dtype),
            swapped(pairs_total.astype(jnp.bfloat16), "seq", level).astype(pairs_total.dtype),
        )
        upper_half = position >> level & 1 == 1
        inflow = inflow + jnp.where(upper_half, other_state, 0.0)
        outflow = outflow + jnp.where(upper_half, 0.0, other_pairs)
        state_total = state_total + other_state
        pairs_total = pairs_total + other_pairs
    before = inflow[None] + jnp.cumsum(key_value, 0) - key_value
    later_state = outflow[None] + own_pairs[None] - jnp.cumsum(query_pairs, 0)
    before_parts = split_state(before)
    later_parts = split_state(later_state)
    scores = jnp.einsum(
        "cthd,cshd->chts", query_blocks, key_blocks, preferred_element_type=jnp.float32
    )
    weights = jnp.where(causal, factor * scores, 0.0).astype(jnp.bfloat16)
    within = jnp.einsum(
        "chts,cshe->cthe", weights, value_blocks, preferred_element_type=jnp.float32
    )
    carried = factor * state_product("cthd,chde->cthe", query_blocks, before_parts)
    attention = (within + carried).astype(jnp.bfloat16).reshape(flat_shape)
    output = lax.psum_scatter(
        lax.dot_general(
            attention, out_weight, (((1,), (1,)), ((), ())), preferred_element_type=jnp.float32
        ).astype(jnp.bfloat16),
        "head",
        scatter_dimension=0,
        tiled=True,
    )
    grad_scores = jnp.einsum(
        "cthe,cshe->chts", grad_blocks, value_blocks, preferred_element_type=jnp.float32
    )
    grad_weights = jnp.where(causal, factor * grad_scores, 0.0).astype(jnp.bfloat16)
    query_grad = jnp.einsum(
        "chts,cshd->cthd", grad_weights, key_blocks, preferred_element_type=jnp.float32
    )
    query_grad = query_grad + factor * state_product("cthe,chde->cthd", grad_blocks, before_parts)
    key_grad = jnp.einsum(
        "chts,cthd->cshd", grad_weights, query_blocks, preferred_element_type=jnp.float32
    )
    key_grad = key_grad + factor * state_product("cshe,chde->cshd", value_blocks, later_parts)
    value_grad = jnp.einsum(
        "chts,cthe->cshe", weights, grad_blocks, preferred_element_type=jnp.float32
    )
    value_grad = value_grad + factor * state_product("cshd,chde->cshe", key_blocks, later_parts)
    weight_grad = lax.psum_scatter(
        lax.dot_general(
            out_grad, attention, (((0,), (0,)), ((), ())), preferred_element_type=jnp.float32
        ),
        "seq",
        scatter_dimension=0,
        tiled=True,
    ) * total_rows ** (-0.5)
    return (
        output,
        query_grad.astype(jnp.bfloat16).reshape(flat_shape),
        key_grad.astype(jnp.bfloat16).reshape(flat_shape),
        value_grad.astype(jnp.bfloat16).reshape(flat_shape),
        weight_grad,
    )


def flipped(position, mask):
    result = position
    for bit in range(mask.bit_length()):
        if mask >> bit & 1:
            step = 1 << bit
            result = result + (1 - 2 * (position // step % 2)) * step
    return result


def nn(a, b):
    return jnp.dot(a, b, preferred_element_type=jnp.float32)


def nt(a, b):
    return lax.dot_general(a, b, (((1,), (1,)), ((), ())), preferred_element_type=jnp.float32)


def tn(a, b):
    return lax.dot_general(a, b, (((0,), (0,)), ((), ())), preferred_element_type=jnp.float32)


def fused_kernel(
    n_seq, n_head, q_hbm, k_hbm, v_hbm, w_hbm, og_hbm,
    out_hbm, qg_hbm, kg_hbm, vg_hbm, wg_hbm,
    out_ref, qg_ref, kg_ref, vg_ref, wg_ref, out_sem,
    q_ref, k_ref, v_ref, w_ref, og_ref, in_sem,
    wf, state_out, state_in, grad, att, att_t, att_in, acc, gathered, out_acc,
    part_out, part_in, sum_out, sum_in,
    z_send, z_recv, p_send, p_recv, c_send, c_recv,
    s_send, s_recv, a_send, a_recv, g_send, g_recv, r_send, r_recv,
):
    rows = q_ref.shape[0]
    width = w_ref.shape[0]
    heads = q_ref.shape[1] // HD
    chips = n_seq // 2
    block = width // n_seq
    mine = rows // n_head
    total_rows = rows * n_seq
    factor = (HD * total_rows) ** (-0.5)
    seq = lax.axis_index("seq")
    z = lax.axis_index("head")
    chip = seq // 2
    core = seq % 2
    partner = chip * 2 + 1 - core

    def zpeer(dz):
        return lax.rem(z + dz, n_head)

    def peer_chip(k):
        return flipped(chip, k)

    def band(j):
        return pl.ds(pl.multiple_of(j * block, block), block)

    def remote(src, dst, send, recv, **where):
        return pltpu.make_async_remote_copy(
            src_ref=src, dst_ref=dst, send_sem=send, recv_sem=recv,
            device_id=where, device_id_type=pl.DeviceIdType.MESH,
        )

    loads = [
        pltpu.make_async_copy(there, here, in_sem.at[at])
        for at, (there, here) in enumerate((
            (k_hbm, k_ref), (v_hbm, v_ref), (og_hbm, og_ref), (w_hbm, w_ref), (q_hbm, q_ref)
        ))
    ]
    for load in loads:
        load.start()
    barrier = pltpu.get_barrier_semaphore()
    for m in range(1, n_seq):
        pl.semaphore_signal(
            barrier, inc=1, device_id={"seq": flipped(seq, m)},
            device_id_type=pl.DeviceIdType.MESH,
        )
    for dz in range(1, n_head):
        pl.semaphore_signal(
            barrier, inc=1, device_id={"head": zpeer(dz)},
            device_id_type=pl.DeviceIdType.MESH,
        )
    pl.semaphore_wait(barrier, n_seq + n_head - 2)

    def z_copy(dz):
        back = n_head - dz
        return remote(
            w_hbm.at[band(seq)], wf.at[back - 1, band(seq)],
            z_send.at[dz - 1], z_recv.at[back - 1], head=zpeer(dz),
        )

    def z_wait(dz):
        return remote(
            w_hbm.at[band(seq)], wf.at[dz - 1, band(seq)],
            z_send.at[dz - 1], z_recv.at[dz - 1], head=zpeer(dz),
        )

    for dz in range(1, n_head):
        z_copy(dz).start()

    def state_copy(m, which):
        return remote(
            state_out.at[which], state_in.at[m - 1],
            s_send.at[m - 1], s_recv.at[m - 1], seq=flipped(seq, m),
        )

    loads[0].wait()
    loads[1].wait()
    for h in range(heads):
        cols = pl.ds(h * HD, HD)
        state_out[0, h] = tn(k_ref[:, cols], v_ref[:, cols]).astype(jnp.bfloat16)
    for m in range(1, n_seq):
        @pl.when(flipped(seq, m) > seq)
        def _():
            state_copy(m, 0).start()

    acc[0] = jnp.zeros(acc.shape[1:], jnp.float32)
    loads[2].wait()
    loads[3].wait()

    @pl.loop(0, n_seq)
    def _(j):
        acc[0] += nn(og_ref[:, band(j)], w_ref[band(j), :])

    grad[...] = acc[0].astype(jnp.bfloat16)
    loads[4].wait()
    for h in range(heads):
        cols = pl.ds(h * HD, HD)
        state_out[1, h] = tn(q_ref[:, cols], grad[:, cols]).astype(jnp.bfloat16)
    for m in range(1, n_seq):
        @pl.when(flipped(seq, m) < seq)
        def _():
            state_copy(m, 1).start()

    row = lax.broadcasted_iota(jnp.int32, (rows, rows), 0)
    col = lax.broadcasted_iota(jnp.int32, (rows, rows), 1)
    for h in range(heads):
        cols = pl.ds(h * HD, HD)
        q, k, v, g = q_ref[:, cols], k_ref[:, cols], v_ref[:, cols], grad[:, cols]
        weights = jnp.where(row >= col, factor * nt(q, k), 0.0).astype(jnp.bfloat16)
        acc[0, :, cols] = nn(weights, v)
        weights = jnp.where(row >= col, factor * nt(g, v), 0.0).astype(jnp.bfloat16)
        acc[1, :, cols] = nn(weights, k)
        weights = jnp.where(row <= col, factor * nt(v, g), 0.0).astype(jnp.bfloat16)
        acc[2, :, cols] = nn(weights, q)
        weights = jnp.where(row <= col, factor * nt(k, q), 0.0).astype(jnp.bfloat16)
        acc[3, :, cols] = nn(weights, g)

    def p_copy(dz, k):
        at = (dz - 1) * chips + k
        return remote(
            wf.at[dz - 1, band(seq)], wf.at[dz - 1, band(seq)],
            p_send.at[at], p_recv.at[at], seq=peer_chip(k) * 2 + core,
        )

    def p_wait(dz, k):
        at = (dz - 1) * chips + k
        there = band(peer_chip(k) * 2 + core)
        return remote(
            wf.at[dz - 1, there], wf.at[dz - 1, there],
            p_send.at[at], p_recv.at[at], seq=peer_chip(k) * 2 + core,
        )

    def c_copy(dz, k, side):
        at = (dz - 1) * chips + k
        there = band(peer_chip(k) * 2 + side)
        return remote(
            wf.at[dz - 1, there], wf.at[dz - 1, there],
            c_send.at[at], c_recv.at[at], seq=partner,
        )

    hops = [1, 3, 2] if n_head == 4 else list(range(1, n_head))

    def forward(dz):
        z_wait(dz).wait_recv()
        for k in range(chips - 1, 0, -1):
            p_copy(dz, k).start()
        c_copy(dz, 0, core).start()

    forward(hops[0])
    inflow = jnp.zeros(state_out.shape[1:], jnp.float32)
    outflow = inflow
    for m in range(1, n_seq):
        state_copy(m, 0).wait_recv()
        arrived = state_in[m - 1].astype(jnp.float32)
        early = (flipped(seq, m) < seq).astype(jnp.float32)
        inflow = inflow + early * arrived
        outflow = outflow + (1.0 - early) * arrived
    inflow = inflow.astype(jnp.bfloat16)
    outflow = outflow.astype(jnp.bfloat16)
    for h in range(heads):
        cols = pl.ds(h * HD, HD)
        full = acc[0, :, cols] + factor * nn(q_ref[:, cols], inflow[h])
        att[:, cols] = full.astype(jnp.bfloat16)
        att_t[cols, :] = full.T.astype(jnp.bfloat16)

    def att_copy(dz):
        back = n_head - dz
        start = pl.multiple_of(zpeer(dz) * mine, mine)
        return remote(
            att.at[pl.ds(start, mine)], att_in.at[back - 1],
            a_send.at[dz - 1], a_recv.at[back - 1], head=zpeer(dz),
        )

    for dz in range(1, n_head):
        att_copy(dz).start()

    def share(j):
        return nn(att_t[...], og_ref[:, band(j)])

    def part_copy(k):
        return remote(
            part_out.at[k], part_in.at[k], g_send.at[k], g_recv.at[k], seq=partner
        )

    def sum_copy(k):
        return remote(
            sum_out.at[k - 1], sum_in.at[k - 1], r_send.at[k - 1], r_recv.at[k - 1],
            seq=peer_chip(k) * 2 + core,
        )

    order = list(range(1, chips))[::-1] + [0]
    for k in order:
        part_out[k] = share(peer_chip(k) * 2 + 1 - core).astype(jnp.bfloat16)
        part_copy(k).start()

    forward(hops[1])
    for k in order:
        part_copy(k).wait_recv()
        total = share(peer_chip(k) * 2 + core) + part_in[k].astype(jnp.float32)
        if k:
            sum_out[k - 1] = total.astype(jnp.bfloat16)
            sum_copy(k).start()
        else:
            gathered[...] = total
    for dz in hops[2:]:
        forward(dz)

    for h in range(heads):
        cols = pl.ds(h * HD, HD)
        q, k, v, g = q_ref[:, cols], k_ref[:, cols], v_ref[:, cols], grad[:, cols]
        qg_ref[:, cols] = (acc[1, :, cols] + factor * nt(g, inflow[h])).astype(jnp.bfloat16)
        kg_ref[:, cols] = (acc[2, :, cols] + factor * nt(v, outflow[h])).astype(jnp.bfloat16)
        vg_ref[:, cols] = (acc[3, :, cols] + factor * nn(k, outflow[h])).astype(jnp.bfloat16)

    stores = [
        pltpu.make_async_copy(here, there, out_sem.at[at])
        for at, (here, there) in enumerate((
            (qg_ref, qg_hbm), (kg_ref, kg_hbm), (vg_ref, vg_hbm),
            (wg_ref, wg_hbm), (out_ref, out_hbm),
        ))
    ]
    for store in stores[:3]:
        store.start()
    for dz in range(1, n_head):
        att_copy(n_head - dz).wait_recv()

    at_home = pl.ds(pl.multiple_of(z * mine, mine), mine)

    @pl.loop(0, n_seq)
    def _(j):
        there = band(j)
        own = nt(att[at_home, :], w_ref[there, :])
        out_acc[:, there] = own.astype(jnp.bfloat16).astype(jnp.float32)

    def add(dz, side):
        @pl.loop(0, chips)
        def _(p):
            there = band(p * 2 + side)
            term = nt(att_in[dz - 1], wf[dz - 1, there, :])
            out_acc[:, there] += term.astype(jnp.bfloat16).astype(jnp.float32)

    def add_other(dz):
        for k in range(chips):
            c_copy(dz, k, 1 - core).wait_recv()
        add(dz, 1 - core)

    for at, dz in enumerate(hops):
        for k in range(1, chips):
            p_wait(dz, k).wait_recv()
            c_copy(dz, k, core).start()
        add(dz, core)
        if at:
            add_other(hops[at - 1])
    for k in range(1, chips):
        sum_copy(k).wait_recv()
        gathered[...] += sum_in[k - 1].astype(jnp.float32)
    wg_ref[...] = (gathered[...] * total_rows ** (-0.5)).T
    stores[3].start()

    add_other(hops[-1])
    out_ref[...] = out_acc[...].astype(jnp.bfloat16)
    stores[4].start()
    for dz in range(1, n_head):
        z_copy(dz).wait_send()
        att_copy(dz).wait_send()
        for k in range(chips):
            if k:
                p_copy(dz, k).wait_send()
            c_copy(dz, k, core).wait_send()
    for m in range(1, n_seq):
        state_copy(m, 0).wait_send()
    for k in range(chips):
        part_copy(k).wait_send()
        if k:
            sum_copy(k).wait_send()
    for store in stores:
        store.wait()


def hand_over(*refs):
    sem = refs[-1]
    copies = [
        pltpu.make_async_copy(refs[at], refs[at + 5], sem.at[at]) for at in range(5)
    ]
    for copy in copies:
        copy.start()
    for copy in copies:
        copy.wait()


def fused(n_seq, n_head, queries, key_rows, value_rows, out_weight, out_grad):
    rows, inner = queries.shape
    width = out_weight.shape[0]
    heads = inner // HD
    chips = n_seq // 2
    block = width // n_seq
    mine = rows // n_head
    bf = jnp.bfloat16
    hbm = pl.BlockSpec(memory_space=pltpu.HBM)

    def sems(count):
        return pltpu.SemaphoreType.DMA((count,))

    others = n_head - 1
    results = pl.pallas_call(
        functools.partial(fused_kernel, n_seq, n_head),
        out_shape=(
            jax.ShapeDtypeStruct((mine, width), bf),
            jax.ShapeDtypeStruct((rows, inner), bf),
            jax.ShapeDtypeStruct((rows, inner), bf),
            jax.ShapeDtypeStruct((rows, inner), bf),
            jax.ShapeDtypeStruct((block, inner), jnp.float32),
        ),
        in_specs=[hbm] * 5,
        out_specs=(hbm,) * 5,
        scratch_shapes=[
            pltpu.VMEM((mine, width), bf),
            pltpu.VMEM((rows, inner), bf),
            pltpu.VMEM((rows, inner), bf),
            pltpu.VMEM((rows, inner), bf),
            pltpu.VMEM((block, inner), jnp.float32),
            sems(5),
            pltpu.VMEM((rows, inner), bf),
            pltpu.VMEM((rows, inner), bf),
            pltpu.VMEM((rows, inner), bf),
            pltpu.VMEM((width, inner), bf),
            pltpu.VMEM((rows, width), bf),
            sems(5),
            pltpu.VMEM((others, width, inner), bf),
            pltpu.VMEM((2, heads, HD, HD), bf),
            pltpu.VMEM((n_seq - 1, heads, HD, HD), bf),
            pltpu.VMEM((rows, inner), bf),
            pltpu.VMEM((rows, inner), bf),
            pltpu.VMEM((inner, rows), bf),
            pltpu.VMEM((others, mine, inner), bf),
            pltpu.VMEM((4, rows, inner), jnp.float32),
            pltpu.VMEM((inner, block), jnp.float32),
            pltpu.VMEM((mine, width), jnp.float32),
            pltpu.VMEM((chips, inner, block), bf),
            pltpu.VMEM((chips, inner, block), bf),
            pltpu.VMEM((chips - 1, inner, block), bf),
            pltpu.VMEM((chips - 1, inner, block), bf),
            sems(others), sems(others),
            sems(others * chips), sems(others * chips),
            sems(others * chips), sems(others * chips),
            sems(n_seq - 1), sems(n_seq - 1),
            sems(others), sems(others),
            sems(chips), sems(chips),
            sems(chips - 1), sems(chips - 1),
        ],
        compiler_params=pltpu.CompilerParams(
            collective_id=0, has_side_effects=True, vmem_limit_bytes=62 << 20
        ),
    )(queries, key_rows, value_rows, out_weight, out_grad)
    return pl.pallas_call(
        hand_over,
        out_shape=tuple(jax.ShapeDtypeStruct(r.shape, r.dtype) for r in results),
        in_specs=[hbm] * 5,
        out_specs=(hbm,) * 5,
        scratch_shapes=[sems(5)],
        compiler_params=pltpu.CompilerParams(vmem_limit_bytes=62 << 20),
    )(*results)


def solution(mesh):
    sizes = (mesh.shape["seq"], mesh.shape["head"])
    body = functools.partial(fused, *sizes) if sizes == (8, 4) else local
    return jax.shard_map(
        body,
        mesh=mesh,
        in_specs=(
            P("seq", "head"),
            P("seq", "head"),
            P("seq", "head"),
            P(None, "head"),
            P("seq", None),
        ),
        out_specs=(
            P(("seq", "head"), None),
            P("seq", "head"),
            P("seq", "head"),
            P("seq", "head"),
            P("seq", "head"),
        ),
        check_vma=False,
    )
```

```python
import functools

import jax
import jax.numpy as jnp
from jax import lax
from jax.experimental import pallas as pl
from jax.experimental.pallas import tpu as pltpu
from jax.sharding import PartitionSpec as P

HD = 128
CH = 64


def swapped(block, axis, distance):
    count = lax.axis_size(axis)
    route = []
    for low in range(count):
        high = low | 1 << distance
        if high != low and high < count:
            route += [(low, high), (high, low)]
    return lax.ppermute(block, axis, route)


def split_state(state):
    upper = state.astype(jnp.bfloat16)
    lower = (state - upper.astype(jnp.float32)).astype(jnp.bfloat16)
    return (upper, lower)


def state_product(form, operand, parts):
    first = jnp.einsum(form, operand, parts[0], preferred_element_type=jnp.float32)
    return first + jnp.einsum(form, operand, parts[1], preferred_element_type=jnp.float32)


def local(queries, key_rows, value_rows, out_weight, out_grad):
    local_rows = queries.shape[0]
    head_count = queries.shape[1] // HD
    blocks = local_rows // CH
    total_rows = local_rows * lax.axis_size("seq")
    factor = (HD * total_rows) ** (-0.5)
    block_shape = (blocks, CH, head_count, HD)
    flat_shape = (local_rows, head_count * HD)
    query_blocks = queries.reshape(block_shape)
    key_blocks = key_rows.reshape(block_shape)
    value_blocks = value_rows.reshape(block_shape)
    causal = (jnp.arange(CH)[:, None] >= jnp.arange(CH)[None, :])[None, None]
    grad_rows = jnp.dot(out_grad, out_weight, preferred_element_type=jnp.float32).astype(
        jnp.bfloat16
    )
    grad_blocks = grad_rows.reshape(block_shape)
    key_value = jnp.einsum(
        "cshd,cshe->chde", key_blocks, value_blocks, preferred_element_type=jnp.float32
    )
    query_pairs = jnp.einsum(
        "cthd,cthe->chde", query_blocks, grad_blocks, preferred_element_type=jnp.float32
    )
    own_state = jnp.sum(key_value, 0)
    own_pairs = jnp.sum(query_pairs, 0)
    empty_state = jnp.zeros_like(own_state)
    position = lax.axis_index("seq")
    level_count = lax.axis_size("seq").bit_length() - 1
    inflow = empty_state
    outflow = empty_state
    state_total = own_state
    pairs_total = own_pairs
    for level in range(level_count):
        other_state, other_pairs = (
            swapped(state_total.astype(jnp.bfloat16), "seq", level).astype(state_total.dtype),
            swapped(pairs_total.astype(jnp.bfloat16), "seq", level).astype(pairs_total.dtype),
        )
        upper_half = position >> level & 1 == 1
        inflow = inflow + jnp.where(upper_half, other_state, 0.0)
        outflow = outflow + jnp.where(upper_half, 0.0, other_pairs)
        state_total = state_total + other_state
        pairs_total = pairs_total + other_pairs
    before = inflow[None] + jnp.cumsum(key_value, 0) - key_value
    later_state = outflow[None] + own_pairs[None] - jnp.cumsum(query_pairs, 0)
    before_parts = split_state(before)
    later_parts = split_state(later_state)
    scores = jnp.einsum(
        "cthd,cshd->chts", query_blocks, key_blocks, preferred_element_type=jnp.float32
    )
    weights = jnp.where(causal, factor * scores, 0.0).astype(jnp.bfloat16)
    within = jnp.einsum(
        "chts,cshe->cthe", weights, value_blocks, preferred_element_type=jnp.float32
    )
    carried = factor * state_product("cthd,chde->cthe", query_blocks, before_parts)
    attention = (within + carried).astype(jnp.bfloat16).reshape(flat_shape)
    output = lax.psum_scatter(
        lax.dot_general(
            attention, out_weight, (((1,), (1,)), ((), ())), preferred_element_type=jnp.float32
        ).astype(jnp.bfloat16),
        "head",
        scatter_dimension=0,
        tiled=True,
    )
    grad_scores = jnp.einsum(
        "cthe,cshe->chts", grad_blocks, value_blocks, preferred_element_type=jnp.float32
    )
    grad_weights = jnp.where(causal, factor * grad_scores, 0.0).astype(jnp.bfloat16)
    query_grad = jnp.einsum(
        "chts,cshd->cthd", grad_weights, key_blocks, preferred_element_type=jnp.float32
    )
    query_grad = query_grad + factor * state_product("cthe,chde->cthd", grad_blocks, before_parts)
    key_grad = jnp.einsum(
        "chts,cthd->cshd", grad_weights, query_blocks, preferred_element_type=jnp.float32
    )
    key_grad = key_grad + factor * state_product("cshe,chde->cshd", value_blocks, later_parts)
    value_grad = jnp.einsum(
        "chts,cthe->cshe", weights, grad_blocks, preferred_element_type=jnp.float32
    )
    value_grad = value_grad + factor * state_product("cshd,chde->cshe", key_blocks, later_parts)
    weight_grad = lax.psum_scatter(
        lax.dot_general(
            out_grad, attention, (((0,), (0,)), ((), ())), preferred_element_type=jnp.float32
        ),
        "seq",
        scatter_dimension=0,
        tiled=True,
    ) * total_rows ** (-0.5)
    return (
        output,
        query_grad.astype(jnp.bfloat16).reshape(flat_shape),
        key_grad.astype(jnp.bfloat16).reshape(flat_shape),
        value_grad.astype(jnp.bfloat16).reshape(flat_shape),
        weight_grad,
    )


def flipped(position, mask):
    result = position
    for bit in range(mask.bit_length()):
        if mask >> bit & 1:
            step = 1 << bit
            result = result + (1 - 2 * (position // step % 2)) * step
    return result


def nn(a, b):
    return jnp.dot(a, b, preferred_element_type=jnp.float32)


def nt(a, b):
    return lax.dot_general(a, b, (((1,), (1,)), ((), ())), preferred_element_type=jnp.float32)


def tn(a, b):
    return lax.dot_general(a, b, (((0,), (0,)), ((), ())), preferred_element_type=jnp.float32)


def fused_kernel(
    n_seq, n_head, q_hbm, k_hbm, v_hbm, w_hbm, og_hbm,
    out_hbm, qg_hbm, kg_hbm, vg_hbm, wg_hbm,
    out_ref, qg_ref, kg_ref, vg_ref, wg_ref, out_sem,
    q_ref, k_ref, v_ref, w_ref, og_ref, in_sem,
    wf, state_out, state_in, grad, att, att_t, att_in, acc, gathered, out_acc,
    part_out, part_in, sum_out, sum_in,
    z_send, z_recv, p_send, p_recv, c_send, c_recv,
    s_send, s_recv, a_send, a_recv, g_send, g_recv, r_send, r_recv,
):
    rows = q_ref.shape[0]
    width = w_ref.shape[0]
    heads = q_ref.shape[1] // HD
    chips = n_seq // 2
    block = width // n_seq
    mine = rows // n_head
    total_rows = rows * n_seq
    factor = (HD * total_rows) ** (-0.5)
    seq = lax.axis_index("seq")
    z = lax.axis_index("head")
    chip = seq // 2
    core = seq % 2
    partner = chip * 2 + 1 - core

    def zpeer(dz):
        return lax.rem(z + dz, n_head)

    def peer_chip(k):
        return flipped(chip, k)

    def band(j):
        return pl.ds(pl.multiple_of(j * block, block), block)

    def remote(src, dst, send, recv, **where):
        return pltpu.make_async_remote_copy(
            src_ref=src, dst_ref=dst, send_sem=send, recv_sem=recv,
            device_id=where, device_id_type=pl.DeviceIdType.MESH,
        )

    loads = [
        pltpu.make_async_copy(there, here, in_sem.at[at])
        for at, (there, here) in enumerate((
            (k_hbm, k_ref), (v_hbm, v_ref), (og_hbm, og_ref), (w_hbm, w_ref), (q_hbm, q_ref)
        ))
    ]
    for load in loads:
        load.start()
    barrier = pltpu.get_barrier_semaphore()
    for m in range(1, n_seq):
        pl.semaphore_signal(
            barrier, inc=1, device_id={"seq": flipped(seq, m)},
            device_id_type=pl.DeviceIdType.MESH,
        )
    for dz in range(1, n_head):
        pl.semaphore_signal(
            barrier, inc=1, device_id={"head": zpeer(dz)},
            device_id_type=pl.DeviceIdType.MESH,
        )
    pl.semaphore_wait(barrier, n_seq + n_head - 2)

    def z_copy(dz):
        back = n_head - dz
        return remote(
            w_hbm.at[band(seq)], wf.at[back - 1, band(seq)],
            z_send.at[dz - 1], z_recv.at[back - 1], head=zpeer(dz),
        )

    def z_wait(dz):
        return remote(
            w_hbm.at[band(seq)], wf.at[dz - 1, band(seq)],
            z_send.at[dz - 1], z_recv.at[dz - 1], head=zpeer(dz),
        )

    for dz in range(1, n_head):
        z_copy(dz).start()

    def state_copy(m, which):
        return remote(
            state_out.at[which], state_in.at[m - 1],
            s_send.at[m - 1], s_recv.at[m - 1], seq=flipped(seq, m),
        )

    loads[0].wait()
    loads[1].wait()
    for h in range(heads):
        cols = pl.ds(h * HD, HD)
        state_out[0, h] = tn(k_ref[:, cols], v_ref[:, cols]).astype(jnp.bfloat16)
    for m in range(1, n_seq):
        @pl.when(flipped(seq, m) > seq)
        def _():
            state_copy(m, 0).start()

    acc[0] = jnp.zeros(acc.shape[1:], jnp.float32)
    loads[2].wait()
    loads[3].wait()

    @pl.loop(0, n_seq)
    def _(j):
        acc[0] += nn(og_ref[:, band(j)], w_ref[band(j), :])

    grad[...] = acc[0].astype(jnp.bfloat16)
    loads[4].wait()
    for h in range(heads):
        cols = pl.ds(h * HD, HD)
        state_out[1, h] = tn(q_ref[:, cols], grad[:, cols]).astype(jnp.bfloat16)
    for m in range(1, n_seq):
        @pl.when(flipped(seq, m) < seq)
        def _():
            state_copy(m, 1).start()

    row = lax.broadcasted_iota(jnp.int32, (rows, rows), 0)
    col = lax.broadcasted_iota(jnp.int32, (rows, rows), 1)
    for h in range(heads):
        cols = pl.ds(h * HD, HD)
        q, k, v, g = q_ref[:, cols], k_ref[:, cols], v_ref[:, cols], grad[:, cols]
        weights = jnp.where(row >= col, factor * nt(q, k), 0.0).astype(jnp.bfloat16)
        acc[0, :, cols] = nn(weights, v)
        weights = jnp.where(row >= col, factor * nt(g, v), 0.0).astype(jnp.bfloat16)
        acc[1, :, cols] = nn(weights, k)
        weights = jnp.where(row <= col, factor * nt(v, g), 0.0).astype(jnp.bfloat16)
        acc[2, :, cols] = nn(weights, q)
        weights = jnp.where(row <= col, factor * nt(k, q), 0.0).astype(jnp.bfloat16)
        acc[3, :, cols] = nn(weights, g)

    def p_copy(dz, k):
        at = (dz - 1) * chips + k
        return remote(
            wf.at[dz - 1, band(seq)], wf.at[dz - 1, band(seq)],
            p_send.at[at], p_recv.at[at], seq=peer_chip(k) * 2 + core,
        )

    def p_wait(dz, k):
        at = (dz - 1) * chips + k
        there = band(peer_chip(k) * 2 + core)
        return remote(
            wf.at[dz - 1, there], wf.at[dz - 1, there],
            p_send.at[at], p_recv.at[at], seq=peer_chip(k) * 2 + core,
        )

    def c_copy(dz, k, side):
        at = (dz - 1) * chips + k
        there = band(peer_chip(k) * 2 + side)
        return remote(
            wf.at[dz - 1, there], wf.at[dz - 1, there],
            c_send.at[at], c_recv.at[at], seq=partner,
        )

    hops = [1, 3, 2] if n_head == 4 else list(range(1, n_head))

    def forward(dz):
        z_wait(dz).wait_recv()
        for k in range(chips - 1, 0, -1):
            p_copy(dz, k).start()
        c_copy(dz, 0, core).start()

    forward(hops[0])
    inflow = jnp.zeros(state_out.shape[1:], jnp.float32)
    outflow = inflow
    for m in range(1, n_seq):
        state_copy(m, 0).wait_recv()
        arrived = state_in[m - 1].astype(jnp.float32)
        early = (flipped(seq, m) < seq).astype(jnp.float32)
        inflow = inflow + early * arrived
        outflow = outflow + (1.0 - early) * arrived
    inflow = inflow.astype(jnp.bfloat16)
    outflow = outflow.astype(jnp.bfloat16)
    for h in range(heads):
        cols = pl.ds(h * HD, HD)
        full = acc[0, :, cols] + factor * nn(q_ref[:, cols], inflow[h])
        att[:, cols] = full.astype(jnp.bfloat16)
        att_t[cols, :] = full.T.astype(jnp.bfloat16)

    def att_copy(dz):
        back = n_head - dz
        start = pl.multiple_of(zpeer(dz) * mine, mine)
        return remote(
            att.at[pl.ds(start, mine)], att_in.at[back - 1],
            a_send.at[dz - 1], a_recv.at[back - 1], head=zpeer(dz),
        )

    for dz in range(1, n_head):
        att_copy(dz).start()

    def share(j):
        return nn(att_t[...], og_ref[:, band(j)])

    def part_copy(k):
        return remote(
            part_out.at[k], part_in.at[k], g_send.at[k], g_recv.at[k], seq=partner
        )

    def sum_copy(k):
        return remote(
            sum_out.at[k - 1], sum_in.at[k - 1], r_send.at[k - 1], r_recv.at[k - 1],
            seq=peer_chip(k) * 2 + core,
        )

    order = list(range(1, chips))[::-1] + [0]
    for k in order:
        part_out[k] = share(peer_chip(k) * 2 + 1 - core).astype(jnp.bfloat16)
        part_copy(k).start()

    forward(hops[1])
    for k in order:
        part_copy(k).wait_recv()
        total = share(peer_chip(k) * 2 + core) + part_in[k].astype(jnp.float32)
        if k:
            sum_out[k - 1] = total.astype(jnp.bfloat16)
            sum_copy(k).start()
        else:
            gathered[...] = total
    for dz in hops[2:]:
        forward(dz)

    for h in range(heads):
        cols = pl.ds(h * HD, HD)
        q, k, v, g = q_ref[:, cols], k_ref[:, cols], v_ref[:, cols], grad[:, cols]
        qg_ref[:, cols] = (acc[1, :, cols] + factor * nt(g, inflow[h])).astype(jnp.bfloat16)
        kg_ref[:, cols] = (acc[2, :, cols] + factor * nt(v, outflow[h])).astype(jnp.bfloat16)
        vg_ref[:, cols] = (acc[3, :, cols] + factor * nn(k, outflow[h])).astype(jnp.bfloat16)

    stores = [
        pltpu.make_async_copy(here, there, out_sem.at[at])
        for at, (here, there) in enumerate((
            (qg_ref, qg_hbm), (kg_ref, kg_hbm), (vg_ref, vg_hbm),
            (wg_ref, wg_hbm), (out_ref, out_hbm),
        ))
    ]
    for store in stores[:3]:
        store.start()
    for dz in range(1, n_head):
        att_copy(n_head - dz).wait_recv()

    at_home = pl.ds(pl.multiple_of(z * mine, mine), mine)

    @pl.loop(0, n_seq)
    def _(j):
        there = band(j)
        own = nt(att[at_home, :], w_ref[there, :])
        out_acc[:, there] = own.astype(jnp.bfloat16).astype(jnp.float32)

    def add(dz, side):
        @pl.loop(0, chips)
        def _(p):
            there = band(p * 2 + side)
            term = nt(att_in[dz - 1], wf[dz - 1, there, :])
            out_acc[:, there] += term.astype(jnp.bfloat16).astype(jnp.float32)

    def add_other(dz):
        for k in range(chips):
            c_copy(dz, k, 1 - core).wait_recv()
        add(dz, 1 - core)

    for at, dz in enumerate(hops):
        for k in range(1, chips):
            p_wait(dz, k).wait_recv()
            c_copy(dz, k, core).start()
        add(dz, core)
        if at:
            add_other(hops[at - 1])
    for k in range(1, chips):
        sum_copy(k).wait_recv()
        gathered[...] += sum_in[k - 1].astype(jnp.float32)
    wg_ref[...] = (gathered[...] * total_rows ** (-0.5)).T
    stores[3].start()

    add_other(hops[-1])
    out_ref[...] = out_acc[...].astype(jnp.bfloat16)
    stores[4].start()
    for dz in range(1, n_head):
        z_copy(dz).wait_send()
        att_copy(dz).wait_send()
        for k in range(chips):
            if k:
                p_copy(dz, k).wait_send()
            c_copy(dz, k, core).wait_send()
    for m in range(1, n_seq):
        state_copy(m, 0).wait_send()
    for k in range(chips):
        part_copy(k).wait_send()
        if k:
            sum_copy(k).wait_send()
    for store in stores:
        store.wait()


def hand_over(*refs):
    sources, targets, held, sem = refs[:5], refs[5:10], refs[10:15], refs[15]
    loads = [
        pltpu.make_async_copy(sources[at], held[at], sem.at[at]) for at in range(5)
    ]
    stores = [
        pltpu.make_async_copy(held[at], targets[at], sem.at[at + 5]) for at in range(5)
    ]
    for load in loads:
        load.start()
    for load, store in zip(loads, stores):
        load.wait()
        store.start()
    for store in stores:
        store.wait()


def fused(n_seq, n_head, queries, key_rows, value_rows, out_weight, out_grad):
    rows, inner = queries.shape
    width = out_weight.shape[0]
    heads = inner // HD
    chips = n_seq // 2
    block = width // n_seq
    mine = rows // n_head
    bf = jnp.bfloat16
    hbm = pl.BlockSpec(memory_space=pltpu.HBM)

    def sems(count):
        return pltpu.SemaphoreType.DMA((count,))

    others = n_head - 1
    results = pl.pallas_call(
        functools.partial(fused_kernel, n_seq, n_head),
        out_shape=(
            jax.ShapeDtypeStruct((mine, width), bf),
            jax.ShapeDtypeStruct((rows, inner), bf),
            jax.ShapeDtypeStruct((rows, inner), bf),
            jax.ShapeDtypeStruct((rows, inner), bf),
            jax.ShapeDtypeStruct((block, inner), jnp.float32),
        ),
        in_specs=[hbm] * 5,
        out_specs=(hbm,) * 5,
        scratch_shapes=[
            pltpu.VMEM((mine, width), bf),
            pltpu.VMEM((rows, inner), bf),
            pltpu.VMEM((rows, inner), bf),
            pltpu.VMEM((rows, inner), bf),
            pltpu.VMEM((block, inner), jnp.float32),
            sems(5),
            pltpu.VMEM((rows, inner), bf),
            pltpu.VMEM((rows, inner), bf),
            pltpu.VMEM((rows, inner), bf),
            pltpu.VMEM((width, inner), bf),
            pltpu.VMEM((rows, width), bf),
            sems(5),
            pltpu.VMEM((others, width, inner), bf),
            pltpu.VMEM((2, heads, HD, HD), bf),
            pltpu.VMEM((n_seq - 1, heads, HD, HD), bf),
            pltpu.VMEM((rows, inner), bf),
            pltpu.VMEM((rows, inner), bf),
            pltpu.VMEM((inner, rows), bf),
            pltpu.VMEM((others, mine, inner), bf),
            pltpu.VMEM((4, rows, inner), jnp.float32),
            pltpu.VMEM((inner, block), jnp.float32),
            pltpu.VMEM((mine, width), jnp.float32),
            pltpu.VMEM((chips, inner, block), bf),
            pltpu.VMEM((chips, inner, block), bf),
            pltpu.VMEM((chips - 1, inner, block), bf),
            pltpu.VMEM((chips - 1, inner, block), bf),
            sems(others), sems(others),
            sems(others * chips), sems(others * chips),
            sems(others * chips), sems(others * chips),
            sems(n_seq - 1), sems(n_seq - 1),
            sems(others), sems(others),
            sems(chips), sems(chips),
            sems(chips - 1), sems(chips - 1),
        ],
        compiler_params=pltpu.CompilerParams(
            collective_id=0, has_side_effects=True, vmem_limit_bytes=62 << 20
        ),
    )(queries, key_rows, value_rows, out_weight, out_grad)
    return pl.pallas_call(
        hand_over,
        out_shape=tuple(jax.ShapeDtypeStruct(r.shape, r.dtype) for r in results),
        in_specs=[hbm] * 5,
        out_specs=(hbm,) * 5,
        scratch_shapes=[pltpu.VMEM(r.shape, r.dtype) for r in results] + [sems(10)],
        compiler_params=pltpu.CompilerParams(vmem_limit_bytes=62 << 20),
    )(*results)


def solution(mesh):
    sizes = (mesh.shape["seq"], mesh.shape["head"])
    body = functools.partial(fused, *sizes) if sizes == (8, 4) else local
    return jax.shard_map(
        body,
        mesh=mesh,
        in_specs=(
            P("seq", "head"),
            P("seq", "head"),
            P("seq", "head"),
            P(None, "head"),
            P("seq", None),
        ),
        out_specs=(
            P(("seq", "head"), None),
            P("seq", "head"),
            P("seq", "head"),
            P("seq", "head"),
            P("seq", "head"),
        ),
        check_vma=False,
    )
```

```python
import functools

import jax
import jax.numpy as jnp
from jax import lax
from jax.experimental import pallas as pl
from jax.experimental.pallas import tpu as pltpu
from jax.sharding import PartitionSpec as P

HD = 128
CH = 64


def swapped(block, axis, distance):
    count = lax.axis_size(axis)
    route = []
    for low in range(count):
        high = low | 1 << distance
        if high != low and high < count:
            route += [(low, high), (high, low)]
    return lax.ppermute(block, axis, route)


def split_state(state):
    upper = state.astype(jnp.bfloat16)
    lower = (state - upper.astype(jnp.float32)).astype(jnp.bfloat16)
    return (upper, lower)


def state_product(form, operand, parts):
    first = jnp.einsum(form, operand, parts[0], preferred_element_type=jnp.float32)
    return first + jnp.einsum(form, operand, parts[1], preferred_element_type=jnp.float32)


def local(queries, key_rows, value_rows, out_weight, out_grad):
    local_rows = queries.shape[0]
    head_count = queries.shape[1] // HD
    blocks = local_rows // CH
    total_rows = local_rows * lax.axis_size("seq")
    factor = (HD * total_rows) ** (-0.5)
    block_shape = (blocks, CH, head_count, HD)
    flat_shape = (local_rows, head_count * HD)
    query_blocks = queries.reshape(block_shape)
    key_blocks = key_rows.reshape(block_shape)
    value_blocks = value_rows.reshape(block_shape)
    causal = (jnp.arange(CH)[:, None] >= jnp.arange(CH)[None, :])[None, None]
    grad_rows = jnp.dot(out_grad, out_weight, preferred_element_type=jnp.float32).astype(
        jnp.bfloat16
    )
    grad_blocks = grad_rows.reshape(block_shape)
    key_value = jnp.einsum(
        "cshd,cshe->chde", key_blocks, value_blocks, preferred_element_type=jnp.float32
    )
    query_pairs = jnp.einsum(
        "cthd,cthe->chde", query_blocks, grad_blocks, preferred_element_type=jnp.float32
    )
    own_state = jnp.sum(key_value, 0)
    own_pairs = jnp.sum(query_pairs, 0)
    empty_state = jnp.zeros_like(own_state)
    position = lax.axis_index("seq")
    level_count = lax.axis_size("seq").bit_length() - 1
    inflow = empty_state
    outflow = empty_state
    state_total = own_state
    pairs_total = own_pairs
    for level in range(level_count):
        other_state, other_pairs = (
            swapped(state_total.astype(jnp.bfloat16), "seq", level).astype(state_total.dtype),
            swapped(pairs_total.astype(jnp.bfloat16), "seq", level).astype(pairs_total.dtype),
        )
        upper_half = position >> level & 1 == 1
        inflow = inflow + jnp.where(upper_half, other_state, 0.0)
        outflow = outflow + jnp.where(upper_half, 0.0, other_pairs)
        state_total = state_total + other_state
        pairs_total = pairs_total + other_pairs
    before = inflow[None] + jnp.cumsum(key_value, 0) - key_value
    later_state = outflow[None] + own_pairs[None] - jnp.cumsum(query_pairs, 0)
    before_parts = split_state(before)
    later_parts = split_state(later_state)
    scores = jnp.einsum(
        "cthd,cshd->chts", query_blocks, key_blocks, preferred_element_type=jnp.float32
    )
    weights = jnp.where(causal, factor * scores, 0.0).astype(jnp.bfloat16)
    within = jnp.einsum(
        "chts,cshe->cthe", weights, value_blocks, preferred_element_type=jnp.float32
    )
    carried = factor * state_product("cthd,chde->cthe", query_blocks, before_parts)
    attention = (within + carried).astype(jnp.bfloat16).reshape(flat_shape)
    output = lax.psum_scatter(
        lax.dot_general(
            attention, out_weight, (((1,), (1,)), ((), ())), preferred_element_type=jnp.float32
        ).astype(jnp.bfloat16),
        "head",
        scatter_dimension=0,
        tiled=True,
    )
    grad_scores = jnp.einsum(
        "cthe,cshe->chts", grad_blocks, value_blocks, preferred_element_type=jnp.float32
    )
    grad_weights = jnp.where(causal, factor * grad_scores, 0.0).astype(jnp.bfloat16)
    query_grad = jnp.einsum(
        "chts,cshd->cthd", grad_weights, key_blocks, preferred_element_type=jnp.float32
    )
    query_grad = query_grad + factor * state_product("cthe,chde->cthd", grad_blocks, before_parts)
    key_grad = jnp.einsum(
        "chts,cthd->cshd", grad_weights, query_blocks, preferred_element_type=jnp.float32
    )
    key_grad = key_grad + factor * state_product("cshe,chde->cshd", value_blocks, later_parts)
    value_grad = jnp.einsum(
        "chts,cthe->cshe", weights, grad_blocks, preferred_element_type=jnp.float32
    )
    value_grad = value_grad + factor * state_product("cshd,chde->cshe", key_blocks, later_parts)
    weight_grad = lax.psum_scatter(
        lax.dot_general(
            out_grad, attention, (((0,), (0,)), ((), ())), preferred_element_type=jnp.float32
        ),
        "seq",
        scatter_dimension=0,
        tiled=True,
    ) * total_rows ** (-0.5)
    return (
        output,
        query_grad.astype(jnp.bfloat16).reshape(flat_shape),
        key_grad.astype(jnp.bfloat16).reshape(flat_shape),
        value_grad.astype(jnp.bfloat16).reshape(flat_shape),
        weight_grad,
    )


def flipped(position, mask):
    result = position
    for bit in range(mask.bit_length()):
        if mask >> bit & 1:
            step = 1 << bit
            result = result + (1 - 2 * (position // step % 2)) * step
    return result


def nn(a, b):
    return jnp.dot(a, b, preferred_element_type=jnp.float32)


def nt(a, b):
    return lax.dot_general(a, b, (((1,), (1,)), ((), ())), preferred_element_type=jnp.float32)


def tn(a, b):
    return lax.dot_general(a, b, (((0,), (0,)), ((), ())), preferred_element_type=jnp.float32)


def fused_kernel(
    n_seq, n_head, q_hbm, k_hbm, v_hbm, w_hbm, og_hbm,
    out_hbm, qg_hbm, kg_hbm, vg_hbm, wg_hbm,
    out_ref, qg_ref, kg_ref, vg_ref, wg_ref, out_sem,
    q_ref, k_ref, v_ref, w_ref, og_ref, in_sem,
    wf, state_out, state_in, grad, att, att_t, att_in, acc, gathered, out_acc,
    part_out, part_in, sum_out, sum_in,
    z_send, z_recv, p_send, p_recv, c_send, c_recv,
    s_send, s_recv, a_send, a_recv, g_send, g_recv, r_send, r_recv,
):
    rows = q_ref.shape[0]
    width = w_ref.shape[0]
    heads = q_ref.shape[1] // HD
    chips = n_seq // 2
    block = width // n_seq
    mine = rows // n_head
    total_rows = rows * n_seq
    factor = (HD * total_rows) ** (-0.5)
    seq = lax.axis_index("seq")
    z = lax.axis_index("head")
    chip = seq // 2
    core = seq % 2
    partner = chip * 2 + 1 - core

    def zpeer(dz):
        return lax.rem(z + dz, n_head)

    def peer_chip(k):
        return flipped(chip, k)

    def band(j):
        return pl.ds(pl.multiple_of(j * block, block), block)

    def remote(src, dst, send, recv, **where):
        return pltpu.make_async_remote_copy(
            src_ref=src, dst_ref=dst, send_sem=send, recv_sem=recv,
            device_id=where, device_id_type=pl.DeviceIdType.MESH,
        )

    loads = [
        pltpu.make_async_copy(there, here, in_sem.at[at])
        for at, (there, here) in enumerate((
            (k_hbm, k_ref), (v_hbm, v_ref), (og_hbm, og_ref), (w_hbm, w_ref), (q_hbm, q_ref)
        ))
    ]
    for load in loads:
        load.start()
    barrier = pltpu.get_barrier_semaphore()
    for m in range(1, n_seq):
        pl.semaphore_signal(
            barrier, inc=1, device_id={"seq": flipped(seq, m)},
            device_id_type=pl.DeviceIdType.MESH,
        )
    for dz in range(1, n_head):
        pl.semaphore_signal(
            barrier, inc=1, device_id={"head": zpeer(dz)},
            device_id_type=pl.DeviceIdType.MESH,
        )
    pl.semaphore_wait(barrier, n_seq + n_head - 2)

    def z_copy(dz):
        back = n_head - dz
        return remote(
            w_hbm.at[band(seq)], wf.at[back - 1, band(seq)],
            z_send.at[dz - 1], z_recv.at[back - 1], head=zpeer(dz),
        )

    def z_wait(dz):
        return remote(
            w_hbm.at[band(seq)], wf.at[dz - 1, band(seq)],
            z_send.at[dz - 1], z_recv.at[dz - 1], head=zpeer(dz),
        )

    for dz in range(1, n_head):
        z_copy(dz).start()

    def state_copy(m, which):
        return remote(
            state_out.at[which], state_in.at[m - 1],
            s_send.at[m - 1], s_recv.at[m - 1], seq=flipped(seq, m),
        )

    loads[0].wait()
    loads[1].wait()
    for h in range(heads):
        cols = pl.ds(h * HD, HD)
        state_out[0, h] = tn(k_ref[:, cols], v_ref[:, cols]).astype(jnp.bfloat16)
    for m in range(1, n_seq):
        @pl.when(flipped(seq, m) > seq)
        def _():
            state_copy(m, 0).start()

    acc[0] = jnp.zeros(acc.shape[1:], jnp.float32)
    loads[2].wait()
    loads[3].wait()

    @pl.loop(0, n_seq)
    def _(j):
        acc[0] += nn(og_ref[:, band(j)], w_ref[band(j), :])

    grad[...] = acc[0].astype(jnp.bfloat16)
    loads[4].wait()
    for h in range(heads):
        cols = pl.ds(h * HD, HD)
        state_out[1, h] = tn(q_ref[:, cols], grad[:, cols]).astype(jnp.bfloat16)
    for m in range(1, n_seq):
        @pl.when(flipped(seq, m) < seq)
        def _():
            state_copy(m, 1).start()

    row = lax.broadcasted_iota(jnp.int32, (rows, rows), 0)
    col = lax.broadcasted_iota(jnp.int32, (rows, rows), 1)
    for h in range(heads):
        cols = pl.ds(h * HD, HD)
        q, k, v, g = q_ref[:, cols], k_ref[:, cols], v_ref[:, cols], grad[:, cols]
        weights = jnp.where(row >= col, factor * nt(q, k), 0.0).astype(jnp.bfloat16)
        acc[0, :, cols] = nn(weights, v)
        weights = jnp.where(row >= col, factor * nt(g, v), 0.0).astype(jnp.bfloat16)
        acc[1, :, cols] = nn(weights, k)
        weights = jnp.where(row <= col, factor * nt(v, g), 0.0).astype(jnp.bfloat16)
        acc[2, :, cols] = nn(weights, q)
        weights = jnp.where(row <= col, factor * nt(k, q), 0.0).astype(jnp.bfloat16)
        acc[3, :, cols] = nn(weights, g)

    def p_copy(dz, k):
        at = (dz - 1) * chips + k
        return remote(
            wf.at[dz - 1, band(seq)], wf.at[dz - 1, band(seq)],
            p_send.at[at], p_recv.at[at], seq=peer_chip(k) * 2 + core,
        )

    def p_wait(dz, k):
        at = (dz - 1) * chips + k
        there = band(peer_chip(k) * 2 + core)
        return remote(
            wf.at[dz - 1, there], wf.at[dz - 1, there],
            p_send.at[at], p_recv.at[at], seq=peer_chip(k) * 2 + core,
        )

    def c_copy(dz, k, side):
        at = (dz - 1) * chips + k
        there = band(peer_chip(k) * 2 + side)
        return remote(
            wf.at[dz - 1, there], wf.at[dz - 1, there],
            c_send.at[at], c_recv.at[at], seq=partner,
        )

    hops = [1, 3, 2] if n_head == 4 else list(range(1, n_head))

    def forward(dz):
        z_wait(dz).wait_recv()
        for k in (2, 1):
            p_copy(dz, k).start()
        c_copy(dz, 0, core).start()

    def half_copy(dz, k, source, target):
        at = (dz - 1) * chips + k
        size = block // 2
        start = (peer_chip(source) * 2 + core) * block + (0 if k else size)
        there = pl.ds(pl.multiple_of(start, size), size)
        return remote(
            wf.at[dz - 1, there], wf.at[dz - 1, there],
            p_send.at[at], p_recv.at[at], seq=peer_chip(target) * 2 + core,
        )

    def relay(dz):
        p_wait(dz, 1).wait_recv()
        half_copy(dz, 3, 1, 2).start()
        c_copy(dz, 1, core).start()
        p_wait(dz, 2).wait_recv()
        half_copy(dz, 0, 2, 1).start()
        c_copy(dz, 2, core).start()

    forward(hops[0])
    inflow = jnp.zeros(state_out.shape[1:], jnp.float32)
    outflow = inflow
    for m in range(1, n_seq):
        state_copy(m, 0).wait_recv()
        arrived = state_in[m - 1].astype(jnp.float32)
        early = (flipped(seq, m) < seq).astype(jnp.float32)
        inflow = inflow + early * arrived
        outflow = outflow + (1.0 - early) * arrived
    inflow = inflow.astype(jnp.bfloat16)
    outflow = outflow.astype(jnp.bfloat16)
    for h in range(heads):
        cols = pl.ds(h * HD, HD)
        full = acc[0, :, cols] + factor * nn(q_ref[:, cols], inflow[h])
        att[:, cols] = full.astype(jnp.bfloat16)
        att_t[cols, :] = full.T.astype(jnp.bfloat16)

    def att_copy(dz):
        back = n_head - dz
        start = pl.multiple_of(zpeer(dz) * mine, mine)
        return remote(
            att.at[pl.ds(start, mine)], att_in.at[back - 1],
            a_send.at[dz - 1], a_recv.at[back - 1], head=zpeer(dz),
        )

    for dz in range(1, n_head):
        att_copy(dz).start()

    def share(j):
        return nn(att_t[...], og_ref[:, band(j)])

    def part_copy(k):
        return remote(
            part_out.at[k], part_in.at[k], g_send.at[k], g_recv.at[k], seq=partner
        )

    def sum_copy(k):
        return remote(
            sum_out.at[k - 1], sum_in.at[k - 1], r_send.at[k - 1], r_recv.at[k - 1],
            seq=peer_chip(k) * 2 + core,
        )

    order = list(range(1, chips))[::-1] + [0]
    for k in order:
        part_out[k] = share(peer_chip(k) * 2 + 1 - core).astype(jnp.bfloat16)
        part_copy(k).start()

    forward(hops[1])
    for k in order:
        part_copy(k).wait_recv()
        total = share(peer_chip(k) * 2 + core) + part_in[k].astype(jnp.float32)
        if k:
            sum_out[k - 1] = total.astype(jnp.bfloat16)
            sum_copy(k).start()
        else:
            gathered[...] = total
    for dz in hops[2:]:
        forward(dz)
    relay(hops[0])

    for h in range(heads):
        cols = pl.ds(h * HD, HD)
        q, k, v, g = q_ref[:, cols], k_ref[:, cols], v_ref[:, cols], grad[:, cols]
        qg_ref[:, cols] = (acc[1, :, cols] + factor * nt(g, inflow[h])).astype(jnp.bfloat16)
        kg_ref[:, cols] = (acc[2, :, cols] + factor * nt(v, outflow[h])).astype(jnp.bfloat16)
        vg_ref[:, cols] = (acc[3, :, cols] + factor * nn(k, outflow[h])).astype(jnp.bfloat16)

    stores = [
        pltpu.make_async_copy(here, there, out_sem.at[at])
        for at, (here, there) in enumerate((
            (qg_ref, qg_hbm), (kg_ref, kg_hbm), (vg_ref, vg_hbm),
            (wg_ref, wg_hbm), (out_ref, out_hbm),
        ))
    ]
    for store in stores[:3]:
        store.start()
    relay(hops[1])
    for dz in range(1, n_head):
        att_copy(n_head - dz).wait_recv()

    at_home = pl.ds(pl.multiple_of(z * mine, mine), mine)

    @pl.loop(0, n_seq)
    def _(j):
        there = band(j)
        own = nt(att[at_home, :], w_ref[there, :])
        out_acc[:, there] = own.astype(jnp.bfloat16).astype(jnp.float32)

    def add(dz, side):
        @pl.loop(0, chips)
        def _(p):
            there = band(p * 2 + side)
            term = nt(att_in[dz - 1], wf[dz - 1, there, :])
            out_acc[:, there] += term.astype(jnp.bfloat16).astype(jnp.float32)

    def add_other(dz):
        for k in range(chips):
            c_copy(dz, k, 1 - core).wait_recv()
        add(dz, 1 - core)

    for dz in hops[2:]:
        relay(dz)
    for at, dz in enumerate(hops):
        half_copy(dz, 3, 3, 2).wait_recv()
        half_copy(dz, 0, 3, 1).wait_recv()
        c_copy(dz, 3, core).start()
        add(dz, core)
        if at:
            add_other(hops[at - 1])
    for k in range(1, chips):
        sum_copy(k).wait_recv()
        gathered[...] += sum_in[k - 1].astype(jnp.float32)
    wg_ref[...] = (gathered[...] * total_rows ** (-0.5)).T
    stores[3].start()

    add_other(hops[-1])
    out_ref[...] = out_acc[...].astype(jnp.bfloat16)
    stores[4].start()
    for dz in range(1, n_head):
        z_copy(dz).wait_send()
        att_copy(dz).wait_send()
        for k in range(chips):
            if k in (1, 2):
                p_copy(dz, k).wait_send()
            else:
                half_copy(dz, k, 1 if k else 2, 2 if k else 1).wait_send()
            c_copy(dz, k, core).wait_send()
    for m in range(1, n_seq):
        state_copy(m, 0).wait_send()
    for k in range(chips):
        part_copy(k).wait_send()
        if k:
            sum_copy(k).wait_send()
    for store in stores:
        store.wait()


def hand_over(*refs):
    sources, targets, held, sem = refs[:5], refs[5:10], refs[10:15], refs[15]
    loads = [
        pltpu.make_async_copy(sources[at], held[at], sem.at[at]) for at in range(5)
    ]
    stores = [
        pltpu.make_async_copy(held[at], targets[at], sem.at[at + 5]) for at in range(5)
    ]
    for load in loads:
        load.start()
    for load, store in zip(loads, stores):
        load.wait()
        store.start()
    for store in stores:
        store.wait()


def fused(n_seq, n_head, queries, key_rows, value_rows, out_weight, out_grad):
    rows, inner = queries.shape
    width = out_weight.shape[0]
    heads = inner // HD
    chips = n_seq // 2
    block = width // n_seq
    mine = rows // n_head
    bf = jnp.bfloat16
    hbm = pl.BlockSpec(memory_space=pltpu.HBM)

    def sems(count):
        return pltpu.SemaphoreType.DMA((count,))

    others = n_head - 1
    results = pl.pallas_call(
        functools.partial(fused_kernel, n_seq, n_head),
        out_shape=(
            jax.ShapeDtypeStruct((mine, width), bf),
            jax.ShapeDtypeStruct((rows, inner), bf),
            jax.ShapeDtypeStruct((rows, inner), bf),
            jax.ShapeDtypeStruct((rows, inner), bf),
            jax.ShapeDtypeStruct((block, inner), jnp.float32),
        ),
        in_specs=[hbm] * 5,
        out_specs=(hbm,) * 5,
        scratch_shapes=[
            pltpu.VMEM((mine, width), bf),
            pltpu.VMEM((rows, inner), bf),
            pltpu.VMEM((rows, inner), bf),
            pltpu.VMEM((rows, inner), bf),
            pltpu.VMEM((block, inner), jnp.float32),
            sems(5),
            pltpu.VMEM((rows, inner), bf),
            pltpu.VMEM((rows, inner), bf),
            pltpu.VMEM((rows, inner), bf),
            pltpu.VMEM((width, inner), bf),
            pltpu.VMEM((rows, width), bf),
            sems(5),
            pltpu.VMEM((others, width, inner), bf),
            pltpu.VMEM((2, heads, HD, HD), bf),
            pltpu.VMEM((n_seq - 1, heads, HD, HD), bf),
            pltpu.VMEM((rows, inner), bf),
            pltpu.VMEM((rows, inner), bf),
            pltpu.VMEM((inner, rows), bf),
            pltpu.VMEM((others, mine, inner), bf),
            pltpu.VMEM((4, rows, inner), jnp.float32),
            pltpu.VMEM((inner, block), jnp.float32),
            pltpu.VMEM((mine, width), jnp.float32),
            pltpu.VMEM((chips, inner, block), bf),
            pltpu.VMEM((chips, inner, block), bf),
            pltpu.VMEM((chips - 1, inner, block), bf),
            pltpu.VMEM((chips - 1, inner, block), bf),
            sems(others), sems(others),
            sems(others * chips), sems(others * chips),
            sems(others * chips), sems(others * chips),
            sems(n_seq - 1), sems(n_seq - 1),
            sems(others), sems(others),
            sems(chips), sems(chips),
            sems(chips - 1), sems(chips - 1),
        ],
        compiler_params=pltpu.CompilerParams(
            collective_id=0, has_side_effects=True, vmem_limit_bytes=62 << 20
        ),
    )(queries, key_rows, value_rows, out_weight, out_grad)
    return pl.pallas_call(
        hand_over,
        out_shape=tuple(jax.ShapeDtypeStruct(r.shape, r.dtype) for r in results),
        in_specs=[hbm] * 5,
        out_specs=(hbm,) * 5,
        scratch_shapes=[pltpu.VMEM(r.shape, r.dtype) for r in results] + [sems(10)],
        compiler_params=pltpu.CompilerParams(vmem_limit_bytes=62 << 20),
    )(*results)


def solution(mesh):
    sizes = (mesh.shape["seq"], mesh.shape["head"])
    body = functools.partial(fused, *sizes) if sizes == (8, 4) else local
    return jax.shard_map(
        body,
        mesh=mesh,
        in_specs=(
            P("seq", "head"),
            P("seq", "head"),
            P("seq", "head"),
            P(None, "head"),
            P("seq", None),
        ),
        out_specs=(
            P(("seq", "head"), None),
            P("seq", "head"),
            P("seq", "head"),
            P("seq", "head"),
            P("seq", "head"),
        ),
        check_vma=False,
    )
```
